32 devices in a mesh: groups: 2 (over x), tensor: 2 (over core), replica: 8 (over z, y).
Axes of the slice: x: 2, y: 2, z: 4, core: 2. Of those that a mesh axis runs over, the one named last changes fastest.
Arguments:
- hidden: bfloat16 [512, 8192], P(('groups', 'replica'), 'tensor'), parts along dimension 0, may hold values from -6 to 6
- base_query_rows: bfloat16 [512, 4096], P(('groups', 'replica'), 'tensor'), parts along dimension 0, may hold values from -110 to 110
- adapter_down_weight: bfloat16 [128, 8192, 64], P(('groups', 'replica'), 'tensor'), parts along dimension 0, may hold values from -0.0625 to 0.0625
- adapter_up_weight: bfloat16 [128, 64, 4096], P(('groups', 'replica'), None, 'tensor'), parts along dimension 0, may hold values from -0.75 to 0.75
- request_adapter: int32 [512], P(('groups', 'replica')), parts along dimension 0, may hold values from 0 to 63, as said below
- adapter_pool_row: int32 [128], P('groups'), parts along dimension 0, may hold values from 0 to 63, as said below
- cached_keys: bfloat16 [512, 192, 512], P(('groups', 'replica'), None, 'tensor'), parts along dimension 0, may hold values from -5 to 5
- cached_values: bfloat16 [512, 192, 512], P(('groups', 'replica'), None, 'tensor'), parts along dimension 0, may hold values from -6 to 6
- request_cache_lengths: int32 [512], P(('groups', 'replica')), parts along dimension 0, may hold values from 48 to 192, as said below
Outputs:
- attended: bfloat16 [512, 4096], P(('groups', 'replica'), 'tensor'), parts along dimension 0
The draws below stay inside these ranges and needn't reach their ends.
There are 2 independent parts, one for each index of `groups`. The reference program is written for one: setup_inputs(seed, part) draws one part's arguments, and reference() takes and returns one part's arrays. A program takes and returns all parts, laid end to end along the dimension named above; each array names one. Nothing has to cross between parts.
Inputs may be any that keep to these rules, and one draw needn't show every extreme that they name: A permutation: adapter a's matrices are row adapter_pool_row[a] of adapter_down_weight and adapter_up_weight. `request_adapter`: in each aligned block of 32 requests, at most 8 requests name adapters whose pool rows lie in one run k * 8 to (k + 1) * 8 - 1; in every block some run is named by exactly 8 requests. `request_cache_lengths`: every aligned block of 32 requests holds a request of 192 positions.
All inputs are finite; a program needn't handle non-finite values.
Results may differ from the reference program's by a relative error of at most 0.0075.
Values may be sent and summed in bfloat16 or wider, within the bound.
A program may use at most 64 MiB of HBM per device.

```python
import jax
import jax.numpy as jnp
from jax import lax

MODEL_WIDTH = 8192
QUERY_HEAD_HALF = 32
KV_HEADS = 4
HEAD_WIDTH = 128
ADAPTER_RANK = 64
EXP_DEV = 8
ROWS_DEV = 32
CACHE_LEN = 192
POOL_ADAPTERS = 64
ROWS = 256
CAP = 8


def pool_order(key):
    return jax.random.permutation(key, POOL_ADAPTERS).astype(jnp.int32)


def key_field(key):
    noise = jax.random.normal(key, (ROWS, CACHE_LEN, KV_HEADS * HEAD_WIDTH), jnp.float32)
    return jnp.clip(noise, -5.0, 5.0)


def draw_adapter_pool_row(key, part):
    return pool_order(key)


def draw_request_adapter(key, part):
    order = pool_order(key)
    holder = jnp.argsort(order).astype(jnp.int32)
    key = jax.random.fold_in(key, 11)
    owners = POOL_ADAPTERS // EXP_DEV
    hot_count = max(owners // 8, 1)
    ranked = jax.random.permutation(jax.random.fold_in(key, 1), owners).astype(jnp.int32)
    hot_rows = jnp.repeat(ranked[:hot_count], CAP)
    cold_slots = jnp.repeat(ranked[hot_count:], CAP)
    cold_need = ROWS_DEV - hot_count * CAP
    blocks = ROWS // ROWS_DEV

    def one_block(block_key):
        chosen = jax.random.permutation(jax.random.fold_in(block_key, 2), cold_slots)[:cold_need]
        owner_rows = jax.random.permutation(jax.random.fold_in(block_key, 3), jnp.concatenate([hot_rows, chosen]))
        within = jax.random.randint(jax.random.fold_in(block_key, 4), (ROWS_DEV,), 0, EXP_DEV)
        return holder[owner_rows * EXP_DEV + within]
    block_keys = jax.random.split(jax.random.fold_in(key, 5), blocks)
    return jax.vmap(one_block)(block_keys).reshape(ROWS).astype(jnp.int32)


def draw_request_cache_lengths(key, part):
    key = jax.random.fold_in(key, 23)
    lengths = jax.random.randint(key, (ROWS,), CACHE_LEN // 4, CACHE_LEN + 1)
    first_rows = jnp.arange(ROWS, dtype=jnp.int32) % ROWS_DEV == 0
    return jnp.where(first_rows, CACHE_LEN, lengths).astype(jnp.int32)


def draw_cached_keys(key, part):
    field = key_field(key)
    return field.astype(jnp.bfloat16)


def draw_base_query_rows(key, part):
    key = jax.random.fold_in(key, 37)
    query_rows = jnp.clip(jax.random.normal(key, (ROWS, QUERY_HEAD_HALF * HEAD_WIDTH), jnp.float32), -5.0, 5.0)
    return query_rows.astype(jnp.bfloat16)


def block_scale(stream_key, extent, shards, smallest, largest):
    loudness, own = 1.0, jax.random.fold_in(stream_key, 6)
    for axis_at, blocks in shards:
        heights = jnp.exp(jax.random.uniform(jax.random.fold_in(own, axis_at), (blocks,), jnp.float32, smallest / len(shards), largest / len(shards)))
        loudness = loudness * jnp.repeat(heights, extent[axis_at] // blocks).reshape([-1 if axis == axis_at else 1 for axis in range(len(extent))])
    return loudness


def gaussian(rng, extent, spread, most, shards=(), kind=jnp.bfloat16):
    loudness = block_scale(rng, extent, shards, -0.22, 0.18) if shards else 1.0
    entries = jax.random.normal(rng, extent, jnp.float32) * spread * loudness
    return jnp.minimum(jnp.maximum(entries, -most), most).astype(kind)


def setup_inputs(seed: int = 0, part: int = 0) -> dict:
    keys = jax.random.split(jax.random.key(seed), 10)
    part_keys = jax.random.split(jax.random.fold_in(keys[9], part), 10)
    hidden = gaussian(part_keys[0], (ROWS, MODEL_WIDTH), 1.0, 6.0, ((0, 8), (1, 2)))
    base_query_rows = draw_base_query_rows(jax.random.fold_in(jax.random.fold_in(keys[9], part), 71), part)
    adapter_down_weight = gaussian(part_keys[2], (POOL_ADAPTERS, MODEL_WIDTH, ADAPTER_RANK), MODEL_WIDTH ** -0.5, 0.0625, ((0, 8), (1, 2)))
    adapter_up_weight = gaussian(part_keys[3], (POOL_ADAPTERS, ADAPTER_RANK, QUERY_HEAD_HALF * HEAD_WIDTH), ADAPTER_RANK ** -0.5, 0.75, ((0, 8), (2, 2)))
    request_adapter = draw_request_adapter(jax.random.fold_in(jax.random.fold_in(keys[9], part), 71), part)
    adapter_pool_row = draw_adapter_pool_row(jax.random.fold_in(jax.random.fold_in(keys[9], part), 71), part)
    cached_keys = draw_cached_keys(jax.random.fold_in(jax.random.fold_in(keys[9], part), 71), part)
    cached_values = gaussian(part_keys[7], (ROWS, CACHE_LEN, KV_HEADS * HEAD_WIDTH), 1.0, 6.0, ((0, 8), (2, 2)))
    request_cache_lengths = draw_request_cache_lengths(jax.random.fold_in(jax.random.fold_in(keys[9], part), 71), part)
    return dict(hidden=hidden, base_query_rows=base_query_rows, adapter_down_weight=adapter_down_weight, adapter_up_weight=adapter_up_weight, request_adapter=request_adapter, adapter_pool_row=adapter_pool_row, cached_keys=cached_keys, cached_values=cached_values, request_cache_lengths=request_cache_lengths)


def attend_rows(query_rows, key_rows, value_rows, request_cache_lengths):
    row_total, cache_size, kv_width = key_rows.shape
    kv_count = kv_width // HEAD_WIDTH
    group_size = query_rows.shape[1] // kv_width
    query_heads = query_rows.reshape(row_total, kv_count, group_size, HEAD_WIDTH).astype(jnp.float32)
    key_heads = key_rows.reshape(row_total, cache_size, kv_count, HEAD_WIDTH).astype(jnp.float32)
    value_heads = value_rows.reshape(row_total, cache_size, kv_count, HEAD_WIDTH).astype(jnp.float32)
    scores = jnp.einsum("rkgd,rlkd->rkgl", query_heads, key_heads) * (HEAD_WIDTH ** -0.5)
    positions = jnp.arange(cache_size, dtype=jnp.int32)
    valid = positions[None, :] < request_cache_lengths[:, None]
    scores = jnp.where(valid[:, None, None, :], scores, jnp.float32(-1e30))
    row_max = jnp.max(scores, axis=-1, keepdims=True)
    expo = jnp.exp(scores - row_max)
    totals = jnp.sum(expo, axis=-1, keepdims=True)
    weights = (expo / totals).astype(jnp.bfloat16)
    result = jnp.einsum("rkgl,rlkd->rkgd", weights.astype(jnp.float32), value_heads)
    return result.astype(jnp.bfloat16).reshape(row_total, kv_count * group_size * HEAD_WIDTH)


def reference(hidden, base_query_rows, adapter_down_weight, adapter_up_weight, request_adapter, adapter_pool_row, cached_keys, cached_values, request_cache_lengths):
    id_table = jnp.arange(POOL_ADAPTERS, dtype=jnp.int32)
    id_hits = request_adapter[:, None] == id_table[None, :]
    pool_index = jnp.sum(jnp.where(id_hits, adapter_pool_row[None, :], 0), axis=1).astype(jnp.int32)
    blocks = ROWS // ROWS_DEV

    def one_block(block_args):
        block_hidden, block_query, current_block_index, block_keys, block_values, block_lengths = block_args
        down_weight_rows = adapter_down_weight[current_block_index].astype(jnp.float32)
        shrink = jnp.einsum("rd,rde->re", block_hidden.astype(jnp.float32), down_weight_rows).astype(jnp.bfloat16)
        up_weight_rows = adapter_up_weight[current_block_index].astype(jnp.float32)
        delta_rows = jnp.einsum("re,req->rq", shrink.astype(jnp.float32), up_weight_rows).astype(jnp.bfloat16)
        query_rows = (block_query.astype(jnp.float32) + delta_rows.astype(jnp.float32)).astype(jnp.bfloat16)
        return attend_rows(query_rows, block_keys, block_values, block_lengths)

    outputs = lax.map(one_block, (
        hidden.reshape(blocks, ROWS_DEV, MODEL_WIDTH),
        base_query_rows.reshape(blocks, ROWS_DEV, QUERY_HEAD_HALF * HEAD_WIDTH),
        pool_index.reshape(blocks, ROWS_DEV),
        cached_keys.reshape(blocks, ROWS_DEV, CACHE_LEN, KV_HEADS * HEAD_WIDTH),
        cached_values.reshape(blocks, ROWS_DEV, CACHE_LEN, KV_HEADS * HEAD_WIDTH),
        request_cache_lengths.reshape(blocks, ROWS_DEV),
    ))
    return outputs.reshape(ROWS, QUERY_HEAD_HALF * HEAD_WIDTH)
```

```python
import functools

import jax
import jax.numpy as jnp
from jax import lax
from jax.experimental import pallas as pl
from jax.experimental.pallas import tpu as pltpu
from jax.sharding import PartitionSpec as P

HEAD_WIDTH = 128
TILE = 16
LANES = 128
F32 = jnp.float32
BF16 = jnp.bfloat16


def iota(shape, axis):
    return lax.broadcasted_iota(jnp.int32, shape, axis)


def to_column(row, size):
    square = iota((size, size), 0) == iota((size, size), 1)
    return jnp.sum(jnp.where(square, row, 0), axis=1, keepdims=True)


def to_row(column, size):
    square = iota((size, size), 0) == iota((size, size), 1)
    return jnp.sum(jnp.where(square, column, 0), axis=0, keepdims=True)


def kernel(
    replicas, holding, rank_width,
    hidden_ref, base_ref, adapter_ref, pool_ref, length_ref,
    down_hbm, up_hbm, key_hbm, value_hbm,
    out_ref,
    down, up, keys, values, send_rows, got_rows, part, other_part,
    send_delta, got_delta, query,
    load_sem, row_send, row_recv, part_sem, delta_send, delta_recv,
):
    rows, width = hidden_ref.shape
    out_width = up.shape[1]
    cap = 2 * rows // replicas
    pieces = TILE // cap
    slots = replicas * TILE
    piece_width = width // pieces
    delta_width = out_width // pieces
    me = lax.axis_index("replica")
    core = lax.axis_index("tensor")

    loads = [
        pltpu.make_async_copy(src, dst, load_sem.at[at])
        for at, (src, dst) in enumerate(
            ((down_hbm, down), (up_hbm, up), (key_hbm, keys), (value_hbm, values))
        )
    ]
    barrier = pltpu.get_barrier_semaphore()
    for off in range(1, replicas):
        pl.semaphore_signal(
            barrier, inc=1, device_id={"replica": lax.rem(me + off, replicas)},
            device_id_type=pl.DeviceIdType.MESH,
        )
    pl.semaphore_signal(
        barrier, inc=1, device_id={"tensor": 1 - core}, device_id_type=pl.DeviceIdType.MESH
    )
    for load in loads:
        load.start()

    adapter_col = to_column(adapter_ref[...], rows)
    pool_row = pool_ref[...]
    pool_size = pool_row.shape[1]
    hits = adapter_col == iota((rows, pool_size), 1)
    index_col = jnp.sum(jnp.where(hits, pool_row, 0), axis=1, keepdims=True)
    owner_col = index_col // holding
    local_col = index_col - owner_col * holding
    owner_row = to_row(owner_col, rows)
    local_row = to_row(local_col, rows)
    same = owner_col == owner_row
    before_i = iota((rows, rows), 1) < iota((rows, rows), 0)
    before_j = iota((rows, rows), 0) < iota((rows, rows), 1)
    place_col = jnp.sum(jnp.where(same & before_i, 1, 0), axis=1, keepdims=True)
    place_row = jnp.sum(jnp.where(same & before_j, 1, 0), axis=0, keepdims=True)

    at_row = iota((slots, rows), 0)
    pick = (owner_row == at_row // TILE) & (place_row == at_row % cap)
    pick_bf = jnp.where(pick, 1.0, 0.0).astype(BF16)
    local_slot = jnp.sum(jnp.where(pick, local_row + 1, 0), axis=1, keepdims=True) - 1
    piece_of = (iota((slots, 1), 0) % TILE) // cap

    step = min(piece_width, 512)
    for start in range(0, piece_width, step):
        taken = None
        for h in range(pieces):
            found = jnp.dot(
                pick_bf, hidden_ref[:, h * piece_width + start:h * piece_width + start + step],
                preferred_element_type=F32,
            )
            taken = found if taken is None else jnp.where(piece_of == h, found, taken)
        send_rows[:, :, start:start + step] = taken.astype(BF16).reshape(replicas, TILE, step)
    send_rows[:, :, piece_width:] = jnp.broadcast_to(
        local_slot.astype(F32), (slots, LANES)
    ).astype(BF16).reshape(replicas, TILE, LANES)

    pl.semaphore_wait(barrier, replicas)

    def exchange(source, target, send_sem, recv_sem):
        copies = []
        order = sorted(range(1, replicas), key=lambda off: abs(off - replicas // 2))
        for off in order:
            there = lax.rem(me + off, replicas)
            copy = pltpu.make_async_remote_copy(
                src_ref=source.at[there], dst_ref=target.at[me],
                send_sem=send_sem.at[off], recv_sem=recv_sem.at[off],
                device_id={"replica": there}, device_id_type=pl.DeviceIdType.MESH,
            )
            copy.start()
            copies.append(copy)
        return copies

    row_copies = exchange(send_rows, got_rows, row_send, row_recv)
    got_rows[me] = send_rows[me]
    loads[0].wait()
    for copy in row_copies:
        copy.wait()

    partial_sum = None
    for h in range(pieces):
        term = lax.dot_general(
            got_rows[:, :, :piece_width].reshape(slots, piece_width),
            down[:, h * piece_width:(h + 1) * piece_width],
            (((1,), (1,)), ((), ())), preferred_element_type=F32,
        )
        partial_sum = term if partial_sum is None else jnp.where(piece_of == h, term, partial_sum)
    local = got_rows[:, :, piece_width:].reshape(slots, LANES).astype(F32)
    per_tile = LANES // rank_width
    tiles = holding * rank_width // LANES
    lane_adapter = (iota((slots, LANES), 1) // rank_width).astype(F32)
    folded = jnp.zeros((slots, LANES), F32)
    for tile in range(tiles):
        keep = local == lane_adapter + tile * per_tile
        folded += jnp.where(keep, partial_sum[:, tile * LANES:(tile + 1) * LANES], 0.0)
    shift = rank_width
    while shift < LANES:
        folded = folded + pltpu.roll(folded, shift, 1)
        shift *= 2
    shift = cap
    row_at = iota((slots, 1), 0)
    while shift < TILE:
        upper = (row_at // shift) % 2 == 1
        folded = folded + jnp.where(
            upper, pltpu.roll(folded, shift, 0), pltpu.roll(folded, slots - shift, 0)
        )
        shift *= 2
    part[...] = folded
    swap = pltpu.make_async_remote_copy(
        src_ref=part, dst_ref=other_part, send_sem=part_sem.at[0], recv_sem=part_sem.at[1],
        device_id={"tensor": 1 - core}, device_id_type=pl.DeviceIdType.MESH,
    )
    swap.start()
    loads[1].wait()
    swap.wait()
    shrink = (part[...] + other_part[...]).astype(BF16).astype(F32)
    wide = jnp.concatenate(
        [
            jnp.where(local == lane_adapter + tile * per_tile, shrink, 0.0).astype(BF16)
            for tile in range(tiles)
        ],
        axis=1,
    )
    step = min(delta_width, 512)
    for start in range(0, delta_width, step):
        taken = None
        for h in range(pieces):
            found = jnp.dot(
                wide, up[:, h * delta_width + start:h * delta_width + start + step],
                preferred_element_type=F32,
            )
            taken = found if taken is None else jnp.where(piece_of == h, found, taken)
        send_delta[:, :, start:start + step] = taken.astype(BF16).reshape(replicas, TILE, step)
    delta_copies = exchange(send_delta, got_delta, delta_send, delta_recv)
    got_delta[me] = send_delta[me]

    at_col = iota((rows, slots), 1)
    mine = (owner_col == at_col // TILE) & (place_col == at_col % cap)
    back = [
        jnp.where(mine & ((at_col % TILE) // cap == h), 1.0, 0.0).astype(BF16)
        for h in range(pieces)
    ]
    loads[2].wait()
    loads[3].wait()
    for copy in delta_copies:
        copy.wait()
    for h in range(pieces):
        columns = slice(h * delta_width, (h + 1) * delta_width)
        delta = jnp.dot(
            back[h], got_delta[...].reshape(slots, delta_width), preferred_element_type=F32
        )
        query[:, columns] = (base_ref[:, columns].astype(F32) + delta).astype(BF16).astype(F32)

    cache_len, kv_width = keys.shape[1:]
    kv_heads = kv_width // HEAD_WIDTH
    heads = out_width // HEAD_WIDTH
    group = heads // kv_heads
    block = 8
    tall = heads * block
    request_of = iota((tall, 1), 0) % block
    kv_of_row = iota((tall, 1), 0) // (group * block)
    length_col = to_column(length_ref[...], rows)
    position = iota((block, cache_len), 1)

    def attend(first):
        loaded = query[first:first + block, :]
        stacked = jnp.concatenate(
            [loaded[:, at * HEAD_WIDTH:(at + 1) * HEAD_WIDTH] for at in range(heads)], axis=0
        )
        spread = jnp.concatenate(
            [jnp.where(kv_of_row == kv, stacked, 0.0).astype(BF16) for kv in range(kv_heads)],
            axis=1,
        )
        scores = None
        for at in range(block):
            found = lax.dot_general(
                spread, keys[first + at], (((1,), (1,)), ((), ())), preferred_element_type=F32
            )
            scores = found if scores is None else jnp.where(request_of == at, found, scores)
        valid = position < length_col[first:first + block, :]
        bias = jnp.where(valid, 0.0, -1e30).astype(F32)
        valid_all = jnp.concatenate([bias] * heads, axis=0)
        scores = jnp.where(valid_all < 0.0, -1e30, scores * (HEAD_WIDTH ** -0.5))
        expo = jnp.exp(scores - jnp.max(scores, axis=1, keepdims=True))
        weights = expo / jnp.sum(expo, axis=1, keepdims=True)
        total = jnp.zeros((tall, kv_width), F32)
        for at in range(block):
            chosen = jnp.where(request_of == at, weights, 0.0).astype(BF16)
            total += jnp.dot(chosen, values[first + at], preferred_element_type=F32)
        return [
            total[at * block:(at + 1) * block,
                  (at // group) * HEAD_WIDTH:(at // group + 1) * HEAD_WIDTH]
            for at in range(heads)
        ]

    for first in range(0, rows, 2 * block):
        low, high = attend(first), attend(first + block)
        for at in range(heads):
            out_ref[first:first + 2 * block, at * HEAD_WIDTH:(at + 1) * HEAD_WIDTH] = (
                jnp.concatenate([low[at], high[at]], axis=0).astype(BF16)
            )


def local_step(
    replicas, hidden, base, down, up, request_adapter, adapter_pool_row, keys, values, lengths
):
    holding, rank_width, out_width = up.shape
    rows, width = hidden.shape
    cap = 2 * rows // replicas
    pieces = TILE // cap
    slots = replicas * TILE
    down_rows = jnp.swapaxes(down, 1, 2).reshape(holding * rank_width, width)
    up_rows = up.reshape(holding * rank_width, out_width)
    vmem = pl.BlockSpec(memory_space=pltpu.VMEM)
    hbm = pl.BlockSpec(memory_space=pl.ANY)
    return pl.pallas_call(
        functools.partial(kernel, replicas, holding, rank_width),
        out_shape=jax.ShapeDtypeStruct((rows, out_width), BF16),
        in_specs=[vmem] * 5 + [hbm] * 4,
        out_specs=vmem,
        scratch_shapes=[
            pltpu.VMEM(down_rows.shape, BF16),
            pltpu.VMEM(up_rows.shape, BF16),
            pltpu.VMEM(keys.shape, BF16),
            pltpu.VMEM(values.shape, BF16),
            pltpu.VMEM((replicas, TILE, width // pieces + LANES), BF16),
            pltpu.VMEM((replicas, TILE, width // pieces + LANES), BF16),
            pltpu.VMEM((slots, LANES), F32),
            pltpu.VMEM((slots, LANES), F32),
            pltpu.VMEM((replicas, TILE, out_width // pieces), BF16),
            pltpu.VMEM((replicas, TILE, out_width // pieces), BF16),
            pltpu.VMEM((rows, out_width), F32),
            pltpu.SemaphoreType.DMA((4,)),
            pltpu.SemaphoreType.DMA((replicas,)),
            pltpu.SemaphoreType.DMA((replicas,)),
            pltpu.SemaphoreType.DMA((2,)),
            pltpu.SemaphoreType.DMA((replicas,)),
            pltpu.SemaphoreType.DMA((replicas,)),
        ],
        compiler_params=pltpu.CompilerParams(
            collective_id=0, has_side_effects=True, vmem_limit_bytes=48 * 1024 * 1024
        ),
        name="adapter_attention",
    )(
        hidden, base, request_adapter.reshape(1, rows),
        adapter_pool_row.reshape(1, adapter_pool_row.shape[0]), lengths.reshape(1, rows),
        down_rows, up_rows, keys, values,
    )


def solution(mesh):
    return jax.shard_map(
        functools.partial(local_step, mesh.shape["replica"]),
        mesh=mesh,
        in_specs=(
            P(("groups", "replica"), "tensor"),
            P(("groups", "replica"), "tensor"),
            P(("groups", "replica"), "tensor", None),
            P(("groups", "replica"), None, "tensor"),
            P(("groups", "replica")),
            P("groups"),
            P(("groups", "replica"), None, "tensor"),
            P(("groups", "replica"), None, "tensor"),
            P(("groups", "replica")),
        ),
        out_specs=P(("groups", "replica"), "tensor"),
        check_vma=False,
    )
```

```python
import functools

import jax
import jax.numpy as jnp
from jax import lax
from jax.experimental import pallas as pl
from jax.experimental.pallas import tpu as pltpu
from jax.sharding import PartitionSpec as P

HEAD_WIDTH = 128
TILE = 16
LANES = 128
F32 = jnp.float32
BF16 = jnp.bfloat16


def iota(shape, axis):
    return lax.broadcasted_iota(jnp.int32, shape, axis)


def to_column(row, size):
    square = iota((size, size), 0) == iota((size, size), 1)
    return jnp.sum(jnp.where(square, row, 0), axis=1, keepdims=True)


def to_row(column, size):
    square = iota((size, size), 0) == iota((size, size), 1)
    return jnp.sum(jnp.where(square, column, 0), axis=0, keepdims=True)


def kernel(
    replicas, holding, rank_width,
    hidden_ref, base_ref, adapter_ref, pool_ref, length_ref,
    down_hbm, up_hbm, key_hbm, value_hbm,
    out_ref,
    down, up, keys, values, send_rows, got_rows, part, other_part,
    send_delta, got_delta, query,
    load_sem, row_send, row_recv, part_sem, delta_send, delta_recv,
):
    rows, width = hidden_ref.shape
    out_width = up.shape[1]
    cap = 2 * rows // replicas
    pieces = TILE // cap
    slots = replicas * TILE
    piece_width = width // pieces
    delta_width = out_width // pieces
    me = lax.axis_index("replica")
    core = lax.axis_index("tensor")

    loads = [
        pltpu.make_async_copy(src, dst, load_sem.at[at])
        for at, (src, dst) in enumerate(
            ((down_hbm, down), (up_hbm, up), (key_hbm, keys), (value_hbm, values))
        )
    ]
    barrier = pltpu.get_barrier_semaphore()
    for off in range(1, replicas):
        pl.semaphore_signal(
            barrier, inc=1, device_id={"replica": lax.rem(me + off, replicas)},
            device_id_type=pl.DeviceIdType.MESH,
        )
    pl.semaphore_signal(
        barrier, inc=1, device_id={"tensor": 1 - core}, device_id_type=pl.DeviceIdType.MESH
    )
    for load in loads:
        load.start()

    adapter_col = to_column(adapter_ref[...], rows)
    pool_row = pool_ref[...]
    pool_size = pool_row.shape[1]
    hits = adapter_col == iota((rows, pool_size), 1)
    index_col = jnp.sum(jnp.where(hits, pool_row, 0), axis=1, keepdims=True)
    owner_col = index_col // holding
    local_col = index_col - owner_col * holding
    owner_row = to_row(owner_col, rows)
    local_row = to_row(local_col, rows)
    same = owner_col == owner_row
    before_i = iota((rows, rows), 1) < iota((rows, rows), 0)
    before_j = iota((rows, rows), 0) < iota((rows, rows), 1)
    place_col = jnp.sum(jnp.where(same & before_i, 1, 0), axis=1, keepdims=True)
    place_row = jnp.sum(jnp.where(same & before_j, 1, 0), axis=0, keepdims=True)

    at_row = iota((slots, rows), 0)
    pick = (owner_row == at_row // TILE) & (place_row == at_row % cap)
    pick_bf = jnp.where(pick, 1.0, 0.0).astype(BF16)
    local_slot = jnp.sum(jnp.where(pick, local_row + 1, 0), axis=1, keepdims=True) - 1
    piece_of = (iota((slots, 1), 0) % TILE) // cap

    step = min(piece_width, 512)
    for start in range(0, piece_width, step):
        taken = None
        for h in range(pieces):
            found = jnp.dot(
                pick_bf, hidden_ref[:, h * piece_width + start:h * piece_width + start + step],
                preferred_element_type=F32,
            )
            taken = found if taken is None else jnp.where(piece_of == h, found, taken)
        send_rows[:, :, start:start + step] = taken.astype(BF16).reshape(replicas, TILE, step)
    send_rows[:, :, piece_width:] = jnp.broadcast_to(
        local_slot.astype(F32), (slots, LANES)
    ).astype(BF16).reshape(replicas, TILE, LANES)

    pl.semaphore_wait(barrier, replicas)

    def exchange(source, target, send_sem, recv_sem):
        copies = []
        order = sorted(range(1, replicas), key=lambda off: abs(off - replicas // 2))
        for off in order:
            there = lax.rem(me + off, replicas)
            copy = pltpu.make_async_remote_copy(
                src_ref=source.at[there], dst_ref=target.at[me],
                send_sem=send_sem.at[off], recv_sem=recv_sem.at[off],
                device_id={"replica": there}, device_id_type=pl.DeviceIdType.MESH,
            )
            copy.start()
            copies.append(copy)
        return copies

    row_copies = exchange(send_rows, got_rows, row_send, row_recv)
    got_rows[me] = send_rows[me]
    loads[0].wait()
    for copy in row_copies:
        copy.wait()

    partial_sum = None
    for h in range(pieces):
        term = lax.dot_general(
            got_rows[:, :, :piece_width].reshape(slots, piece_width),
            down[:, h * piece_width:(h + 1) * piece_width],
            (((1,), (1,)), ((), ())), preferred_element_type=F32,
        )
        partial_sum = term if partial_sum is None else jnp.where(piece_of == h, term, partial_sum)
    local = got_rows[:, :, piece_width:].reshape(slots, LANES).astype(F32)
    per_tile = LANES // rank_width
    tiles = holding * rank_width // LANES
    lane_adapter = (iota((slots, LANES), 1) // rank_width).astype(F32)
    folded = jnp.zeros((slots, LANES), F32)
    for tile in range(tiles):
        keep = local == lane_adapter + tile * per_tile
        folded += jnp.where(keep, partial_sum[:, tile * LANES:(tile + 1) * LANES], 0.0)
    shift = rank_width
    while shift < LANES:
        folded = folded + pltpu.roll(folded, shift, 1)
        shift *= 2
    shift = cap
    row_at = iota((slots, 1), 0)
    while shift < TILE:
        upper = (row_at // shift) % 2 == 1
        folded = folded + jnp.where(
            upper, pltpu.roll(folded, shift, 0), pltpu.roll(folded, slots - shift, 0)
        )
        shift *= 2
    part[...] = folded
    swap = pltpu.make_async_remote_copy(
        src_ref=part, dst_ref=other_part, send_sem=part_sem.at[0], recv_sem=part_sem.at[1],
        device_id={"tensor": 1 - core}, device_id_type=pl.DeviceIdType.MESH,
    )
    swap.start()
    loads[1].wait()
    swap.wait()
    shrink = (part[...] + other_part[...]).astype(BF16).astype(F32)
    wide = jnp.concatenate(
        [
            jnp.where(local == lane_adapter + tile * per_tile, shrink, 0.0).astype(BF16)
            for tile in range(tiles)
        ],
        axis=1,
    )
    step = min(delta_width, 512)
    for start in range(0, delta_width, step):
        taken = None
        for h in range(pieces):
            found = jnp.dot(
                wide, up[:, h * delta_width + start:h * delta_width + start + step],
                preferred_element_type=F32,
            )
            taken = found if taken is None else jnp.where(piece_of == h, found, taken)
        send_delta[:, :, start:start + step] = taken.astype(BF16).reshape(replicas, TILE, step)
    delta_copies = exchange(send_delta, got_delta, delta_send, delta_recv)
    got_delta[me] = send_delta[me]

    at_col = iota((rows, slots), 1)
    mine = (owner_col == at_col // TILE) & (place_col == at_col % cap)
    back = [
        jnp.where(mine & ((at_col % TILE) // cap == h), 1.0, 0.0).astype(BF16)
        for h in range(pieces)
    ]
    loads[2].wait()
    loads[3].wait()
    for copy in delta_copies:
        copy.wait()
    for h in range(pieces):
        columns = slice(h * delta_width, (h + 1) * delta_width)
        delta = jnp.dot(
            back[h], got_delta[...].reshape(slots, delta_width), preferred_element_type=F32
        )
        query[:, columns] = (base_ref[:, columns].astype(F32) + delta).astype(BF16).astype(F32)

    cache_len, kv_width = keys.shape[1:]
    kv_heads = kv_width // HEAD_WIDTH
    heads = out_width // HEAD_WIDTH
    group = heads // kv_heads
    block = 8
    tall = heads * block
    request_of = iota((tall, 1), 0) % block
    kv_of_row = iota((tall, 1), 0) // (group * block)
    length_col = to_column(length_ref[...], rows)
    position = iota((block, cache_len), 1)

    def attend(first):
        loaded = query[first:first + block, :]
        stacked = jnp.concatenate(
            [loaded[:, at * HEAD_WIDTH:(at + 1) * HEAD_WIDTH] for at in range(heads)], axis=0
        )
        spread = jnp.concatenate(
            [jnp.where(kv_of_row == kv, stacked, 0.0).astype(BF16) for kv in range(kv_heads)],
            axis=1,
        )
        scores = None
        for at in range(block):
            found = lax.dot_general(
                spread, keys[first + at], (((1,), (1,)), ((), ())), preferred_element_type=F32
            )
            scores = found if scores is None else jnp.where(request_of == at, found, scores)
        valid = position < length_col[first:first + block, :]
        bias = jnp.where(valid, 0.0, -1e30).astype(F32)
        valid_all = jnp.concatenate([bias] * heads, axis=0)
        scores = jnp.where(valid_all < 0.0, -1e30, scores * (HEAD_WIDTH ** -0.5))
        expo = jnp.exp(scores - jnp.max(scores, axis=1, keepdims=True))
        weights = expo / jnp.sum(expo, axis=1, keepdims=True)
        total = jnp.zeros((tall, kv_width), F32)
        for at in range(block):
            chosen = jnp.where(request_of == at, weights, 0.0).astype(BF16)
            total += jnp.dot(chosen, values[first + at], preferred_element_type=F32)
        return [
            total[at * block:(at + 1) * block,
                  (at // group) * HEAD_WIDTH:(at // group + 1) * HEAD_WIDTH]
            for at in range(heads)
        ]

    for first in range(0, rows, 2 * block):
        low, high = attend(first), attend(first + block)
        for at in range(heads):
            out_ref[first:first + 2 * block, at * HEAD_WIDTH:(at + 1) * HEAD_WIDTH] = (
                jnp.concatenate([low[at], high[at]], axis=0).astype(BF16)
            )


def local_step(
    replicas, hidden, base, down, up, request_adapter, adapter_pool_row, keys, values, lengths
):
    holding, rank_width, out_width = up.shape
    rows, width = hidden.shape
    cap = 2 * rows // replicas
    pieces = TILE // cap
    slots = replicas * TILE
    down_rows = jnp.swapaxes(down, 1, 2).reshape(holding * rank_width, width)
    up_rows = up.reshape(holding * rank_width, out_width)
    vmem = pl.BlockSpec(memory_space=pltpu.VMEM)
    hbm = pl.BlockSpec(memory_space=pl.ANY)
    return pl.pallas_call(
        functools.partial(kernel, replicas, holding, rank_width),
        out_shape=jax.ShapeDtypeStruct((rows, out_width), BF16),
        in_specs=[vmem] * 5 + [hbm] * 4,
        out_specs=vmem,
        scratch_shapes=[
            pltpu.VMEM(down_rows.shape, BF16),
            pltpu.VMEM(up_rows.shape, BF16),
            pltpu.VMEM(keys.shape, BF16),
            pltpu.VMEM(values.shape, BF16),
            pltpu.VMEM((replicas, TILE, width // pieces + LANES), BF16),
            pltpu.VMEM((replicas, TILE, width // pieces + LANES), BF16),
            pltpu.VMEM((slots, LANES), F32),
            pltpu.VMEM((slots, LANES), F32),
            pltpu.VMEM((replicas, TILE, out_width // pieces), BF16),
            pltpu.VMEM((replicas, TILE, out_width // pieces), BF16),
            pltpu.VMEM((rows, out_width), F32),
            pltpu.SemaphoreType.DMA((4,)),
            pltpu.SemaphoreType.DMA((replicas,)),
            pltpu.SemaphoreType.DMA((replicas,)),
            pltpu.SemaphoreType.DMA((2,)),
            pltpu.SemaphoreType.DMA((replicas,)),
            pltpu.SemaphoreType.DMA((replicas,)),
        ],
        compiler_params=pltpu.CompilerParams(
            collective_id=0, has_side_effects=True, vmem_limit_bytes=63 * 1024 * 1024
        ),
        name="adapter_attention",
    )(
        hidden, base, request_adapter.reshape(1, rows),
        adapter_pool_row.reshape(1, adapter_pool_row.shape[0]), lengths.reshape(1, rows),
        down_rows, up_rows, keys, values,
    )


def solution(mesh):
    return jax.shard_map(
        functools.partial(local_step, mesh.shape["replica"]),
        mesh=mesh,
        in_specs=(
            P(("groups", "replica"), "tensor"),
            P(("groups", "replica"), "tensor"),
            P(("groups", "replica"), "tensor", None),
            P(("groups", "replica"), None, "tensor"),
            P(("groups", "replica")),
            P("groups"),
            P(("groups", "replica"), None, "tensor"),
            P(("groups", "replica"), None, "tensor"),
            P(("groups", "replica")),
        ),
        out_specs=P(("groups", "replica"), "tensor"),
        check_vma=False,
    )
```

```python
import functools

import jax
import jax.numpy as jnp
from jax import lax
from jax.experimental import pallas as pl
from jax.experimental.pallas import tpu as pltpu
from jax.sharding import PartitionSpec as P

HEAD_WIDTH = 128
TILE = 16
LANES = 128
PARTS = 2
F32 = jnp.float32
BF16 = jnp.bfloat16


def iota(shape, axis):
    return lax.broadcasted_iota(jnp.int32, shape, axis)


def to_column(row, size):
    square = iota((size, size), 0) == iota((size, size), 1)
    return jnp.sum(jnp.where(square, row, 0), axis=1, keepdims=True)


def to_row(column, size):
    square = iota((size, size), 0) == iota((size, size), 1)
    return jnp.sum(jnp.where(square, column, 0), axis=0, keepdims=True)


def kernel(
    replicas, holding, rank_width,
    hidden_ref, base_ref, adapter_ref, pool_ref, length_ref,
    down_hbm, up_hbm, key_hbm, value_hbm,
    out_ref,
    down, up, keys, values, send_rows, got_rows, part, other_part,
    send_delta, got_delta, query,
    load_sem, row_send, row_recv, part_sem, delta_send, delta_recv,
):
    rows, width = hidden_ref.shape
    out_width = up.shape[1]
    parts = send_rows.shape[0]
    cap = 2 * rows // replicas // parts
    pieces = TILE // cap
    slots = replicas * TILE
    piece_width = width // pieces
    delta_width = out_width // pieces
    me = lax.axis_index("replica")
    core = lax.axis_index("tensor")

    loads = [
        pltpu.make_async_copy(src, dst, load_sem.at[at])
        for at, (src, dst) in enumerate(
            ((down_hbm, down), (up_hbm, up), (key_hbm, keys), (value_hbm, values))
        )
    ]
    barrier = pltpu.get_barrier_semaphore()
    for off in range(1, replicas):
        pl.semaphore_signal(
            barrier, inc=1, device_id={"replica": lax.rem(me + off, replicas)},
            device_id_type=pl.DeviceIdType.MESH,
        )
    pl.semaphore_signal(
        barrier, inc=1, device_id={"tensor": 1 - core}, device_id_type=pl.DeviceIdType.MESH
    )
    for load in loads:
        load.start()

    adapter_col = to_column(adapter_ref[...], rows)
    pool_row = pool_ref[...]
    pool_size = pool_row.shape[1]
    hits = adapter_col == iota((rows, pool_size), 1)
    index_col = jnp.sum(jnp.where(hits, pool_row, 0), axis=1, keepdims=True)
    owner_col = index_col // holding
    local_col = index_col - owner_col * holding
    owner_row = to_row(owner_col, rows)
    local_row = to_row(local_col, rows)
    same = owner_col == owner_row
    before_i = iota((rows, rows), 1) < iota((rows, rows), 0)
    before_j = iota((rows, rows), 0) < iota((rows, rows), 1)
    place_col = jnp.sum(jnp.where(same & before_i, 1, 0), axis=1, keepdims=True)
    place_row = jnp.sum(jnp.where(same & before_j, 1, 0), axis=0, keepdims=True)

    at_row = iota((slots, rows), 0)
    piece_of = (iota((slots, 1), 0) % TILE) // cap
    step = min(piece_width, 512)

    def fill(number):
        pick = (owner_row == at_row // TILE) & (place_row == at_row % cap + number * cap)
        pick_pieces = jnp.concatenate(
            [
                jnp.where(pick & ((at_row % TILE) // cap == h), 1.0, 0.0).astype(BF16)
                for h in range(pieces)
            ],
            axis=1,
        )
        local_slot = jnp.sum(jnp.where(pick, local_row + 1, 0), axis=1, keepdims=True) - 1
        for start in range(0, piece_width, step):
            stacked = jnp.concatenate(
                [
                    hidden_ref[:, h * piece_width + start:h * piece_width + start + step]
                    for h in range(pieces)
                ],
                axis=0,
            )
            taken = jnp.dot(pick_pieces, stacked, preferred_element_type=F32)
            send_rows[number, :, :, start:start + step] = taken.astype(BF16).reshape(
                replicas, TILE, step
            )
        send_rows[number, :, :, piece_width:] = jnp.broadcast_to(
            local_slot.astype(F32), (slots, LANES)
        ).astype(BF16).reshape(replicas, TILE, LANES)

    def exchange(number, source, target, send_sem, recv_sem):
        copies = []
        order = sorted(range(1, replicas), key=lambda off: abs(off - replicas // 2))
        for off in order:
            there = lax.rem(me + off, replicas)
            copy = pltpu.make_async_remote_copy(
                src_ref=source.at[number, there], dst_ref=target.at[number, me],
                send_sem=send_sem.at[number, off], recv_sem=recv_sem.at[number, off],
                device_id={"replica": there}, device_id_type=pl.DeviceIdType.MESH,
            )
            copy.start()
            copies.append(copy)
        target[number, me] = source[number, me]
        return copies

    per_tile = LANES // rank_width
    tiles = holding * rank_width // LANES
    lane_adapter = (iota((slots, LANES), 1) // rank_width).astype(F32)
    row_at = iota((slots, 1), 0)

    def shrink_part(number):
        partial_sum = None
        for h in range(pieces):
            term = lax.dot_general(
                got_rows[number, :, :, :piece_width].reshape(slots, piece_width),
                down[:, h * piece_width:(h + 1) * piece_width],
                (((1,), (1,)), ((), ())), preferred_element_type=F32,
            )
            partial_sum = (
                term if partial_sum is None else jnp.where(piece_of == h, term, partial_sum)
            )
        local = got_rows[number, :, :, piece_width:].reshape(slots, LANES).astype(F32)
        folded = jnp.zeros((slots, LANES), F32)
        for tile in range(tiles):
            keep = local == lane_adapter + tile * per_tile
            folded += jnp.where(keep, partial_sum[:, tile * LANES:(tile + 1) * LANES], 0.0)
        shift = rank_width
        while shift < LANES:
            folded = folded + pltpu.roll(folded, shift, 1)
            shift *= 2
        shift = cap
        while shift < TILE:
            upper = (row_at // shift) % 2 == 1
            folded = folded + jnp.where(
                upper, pltpu.roll(folded, shift, 0), pltpu.roll(folded, slots - shift, 0)
            )
            shift *= 2
        part[number] = folded
        swap = pltpu.make_async_remote_copy(
            src_ref=part.at[number], dst_ref=other_part.at[number],
            send_sem=part_sem.at[number, 0], recv_sem=part_sem.at[number, 1],
            device_id={"tensor": 1 - core}, device_id_type=pl.DeviceIdType.MESH,
        )
        swap.start()
        return swap

    def expand_part(number):
        local = got_rows[number, :, :, piece_width:].reshape(slots, LANES).astype(F32)
        shrink = (part[number] + other_part[number]).astype(BF16).astype(F32)
        wide = jnp.concatenate(
            [
                jnp.where(local == lane_adapter + tile * per_tile, shrink, 0.0).astype(BF16)
                for tile in range(tiles)
            ],
            axis=1,
        )
        wide_step = min(delta_width, 512)
        for start in range(0, delta_width, wide_step):
            taken = None
            for h in range(pieces):
                found = jnp.dot(
                    wide, up[:, h * delta_width + start:h * delta_width + start + wide_step],
                    preferred_element_type=F32,
                )
                taken = found if taken is None else jnp.where(piece_of == h, found, taken)
            send_delta[number, :, :, start:start + wide_step] = taken.astype(BF16).reshape(
                replicas, TILE, wide_step
            )

    fill(0)
    pl.semaphore_wait(barrier, replicas)
    row_copies = []
    for number in range(parts):
        if number:
            fill(number)
        row_copies.append(exchange(number, send_rows, got_rows, row_send, row_recv))
    delta_copies, swaps = [], []
    for number in range(parts):
        for copy in row_copies[number]:
            copy.wait_recv()
        if number == 0:
            loads[0].wait()
        swap = shrink_part(number)
        if number == 0:
            loads[1].wait()
        swap.wait_recv()
        swaps.append(swap)
        expand_part(number)
        delta_copies.append(exchange(number, send_delta, got_delta, delta_send, delta_recv))

    at_col = iota((rows, slots), 1)
    loads[2].wait()
    loads[3].wait()
    deltas = [None] * pieces
    for number in range(parts):
        mine = (owner_col == at_col // TILE) & (place_col == at_col % cap + number * cap)
        for copy in delta_copies[number]:
            copy.wait_recv()
        for h in range(pieces):
            back = jnp.where(mine & ((at_col % TILE) // cap == h), 1.0, 0.0).astype(BF16)
            found = jnp.dot(
                back, got_delta[number].reshape(slots, delta_width), preferred_element_type=F32
            )
            deltas[h] = found if deltas[h] is None else deltas[h] + found
    for h in range(pieces):
        columns = slice(h * delta_width, (h + 1) * delta_width)
        query[:, columns] = (base_ref[:, columns].astype(F32) + deltas[h]).astype(BF16).astype(F32)
    for copy in sum(row_copies, []) + sum(delta_copies, []) + swaps:
        copy.wait_send()

    cache_len, kv_width = keys.shape[1:]
    kv_heads = kv_width // HEAD_WIDTH
    heads = out_width // HEAD_WIDTH
    group = heads // kv_heads
    block = 8
    tall = heads * block
    request_of = iota((tall, 1), 0) % block
    kv_of_row = iota((tall, 1), 0) // (group * block)
    length_col = to_column(length_ref[...], rows)
    position = iota((block, cache_len), 1)

    def attend(first):
        loaded = query[first:first + block, :]
        stacked = jnp.concatenate(
            [loaded[:, at * HEAD_WIDTH:(at + 1) * HEAD_WIDTH] for at in range(heads)], axis=0
        )
        spread = jnp.concatenate(
            [jnp.where(kv_of_row == kv, stacked, 0.0).astype(BF16) for kv in range(kv_heads)],
            axis=1,
        )
        scores = None
        for at in range(block):
            found = lax.dot_general(
                spread, keys[first + at], (((1,), (1,)), ((), ())), preferred_element_type=F32
            )
            scores = found if scores is None else jnp.where(request_of == at, found, scores)
        valid = position < length_col[first:first + block, :]
        bias = jnp.where(valid, 0.0, -1e30).astype(F32)
        valid_all = jnp.concatenate([bias] * heads, axis=0)
        scores = jnp.where(valid_all < 0.0, -1e30, scores * (HEAD_WIDTH ** -0.5))
        expo = jnp.exp(scores - jnp.max(scores, axis=1, keepdims=True))
        weights = expo / jnp.sum(expo, axis=1, keepdims=True)
        total = jnp.zeros((tall, kv_width), F32)
        for at in range(block):
            chosen = jnp.where(request_of == at, weights, 0.0).astype(BF16)
            total += jnp.dot(chosen, values[first + at], preferred_element_type=F32)
        return [
            total[at * block:(at + 1) * block,
                  (at // group) * HEAD_WIDTH:(at // group + 1) * HEAD_WIDTH]
            for at in range(heads)
        ]

    for first in range(0, rows, 2 * block):
        low, high = attend(first), attend(first + block)
        for at in range(heads):
            out_ref[first:first + 2 * block, at * HEAD_WIDTH:(at + 1) * HEAD_WIDTH] = (
                jnp.concatenate([low[at], high[at]], axis=0).astype(BF16)
            )


def local_step(
    replicas, hidden, base, down, up, request_adapter, adapter_pool_row, keys, values, lengths
):
    holding, rank_width, out_width = up.shape
    rows, width = hidden.shape
    parts = min(PARTS, 2 * rows // replicas)
    cap = 2 * rows // replicas // parts
    pieces = TILE // cap
    slots = replicas * TILE
    down_rows = jnp.swapaxes(down, 1, 2).reshape(holding * rank_width, width)
    up_rows = up.reshape(holding * rank_width, out_width)
    vmem = pl.BlockSpec(memory_space=pltpu.VMEM)
    hbm = pl.BlockSpec(memory_space=pl.ANY)
    return pl.pallas_call(
        functools.partial(kernel, replicas, holding, rank_width),
        out_shape=jax.ShapeDtypeStruct((rows, out_width), BF16),
        in_specs=[vmem] * 5 + [hbm] * 4,
        out_specs=vmem,
        scratch_shapes=[
            pltpu.VMEM(down_rows.shape, BF16),
            pltpu.VMEM(up_rows.shape, BF16),
            pltpu.VMEM(keys.shape, BF16),
            pltpu.VMEM(values.shape, BF16),
            pltpu.VMEM((parts, replicas, TILE, width // pieces + LANES), BF16),
            pltpu.VMEM((parts, replicas, TILE, width // pieces + LANES), BF16),
            pltpu.VMEM((parts, slots, LANES), F32),
            pltpu.VMEM((parts, slots, LANES), F32),
            pltpu.VMEM((parts, replicas, TILE, out_width // pieces), BF16),
            pltpu.VMEM((parts, replicas, TILE, out_width // pieces), BF16),
            pltpu.VMEM((rows, out_width), F32),
            pltpu.SemaphoreType.DMA((4,)),
            pltpu.SemaphoreType.DMA((parts, replicas)),
            pltpu.SemaphoreType.DMA((parts, replicas)),
            pltpu.SemaphoreType.DMA((parts, 2)),
            pltpu.SemaphoreType.DMA((parts, replicas)),
            pltpu.SemaphoreType.DMA((parts, replicas)),
        ],
        compiler_params=pltpu.CompilerParams(
            collective_id=0, has_side_effects=True, vmem_limit_bytes=63 * 1024 * 1024
        ),
        name="adapter_attention",
    )(
        hidden, base, request_adapter.reshape(1, rows),
        adapter_pool_row.reshape(1, adapter_pool_row.shape[0]), lengths.reshape(1, rows),
        down_rows, up_rows, keys, values,
    )


def solution(mesh):
    return jax.shard_map(
        functools.partial(local_step, mesh.shape["replica"]),
        mesh=mesh,
        in_specs=(
            P(("groups", "replica"), "tensor"),
            P(("groups", "replica"), "tensor"),
            P(("groups", "replica"), "tensor", None),
            P(("groups", "replica"), None, "tensor"),
            P(("groups", "replica")),
            P("groups"),
            P(("groups", "replica"), None, "tensor"),
            P(("groups", "replica"), None, "tensor"),
            P(("groups", "replica")),
        ),
        out_specs=P(("groups", "replica"), "tensor"),
        check_vma=False,
    )
```

```python
import functools

import jax
import jax.numpy as jnp
from jax import lax
from jax.experimental import pallas as pl
from jax.experimental.pallas import tpu as pltpu
from jax.sharding import PartitionSpec as P

HEAD_WIDTH = 128
TILE = 16
LANES = 128
PARTS = 1
F32 = jnp.float32
BF16 = jnp.bfloat16


def iota(shape, axis):
    return lax.broadcasted_iota(jnp.int32, shape, axis)


def to_column(row, size):
    square = iota((size, size), 0) == iota((size, size), 1)
    return jnp.sum(jnp.where(square, row, 0), axis=1, keepdims=True)


def to_row(column, size):
    square = iota((size, size), 0) == iota((size, size), 1)
    return jnp.sum(jnp.where(square, column, 0), axis=0, keepdims=True)


def kernel(
    replicas, holding, rank_width,
    hidden_ref, base_ref, adapter_ref, pool_ref, length_ref,
    down_hbm, up_hbm, key_hbm, value_hbm,
    out_ref,
    down, up, keys, values, send_rows, got_rows, part, other_part,
    send_delta, got_delta, query,
    load_sem, row_send, row_recv, part_sem, delta_send, delta_recv,
):
    rows, width = hidden_ref.shape
    out_width = up.shape[1]
    parts = send_rows.shape[0]
    cap = 2 * rows // replicas // parts
    pieces = TILE // cap
    slots = replicas * TILE
    piece_width = width // pieces
    delta_width = out_width // pieces
    me = lax.axis_index("replica")
    core = lax.axis_index("tensor")

    loads = [
        pltpu.make_async_copy(src, dst, load_sem.at[at])
        for at, (src, dst) in enumerate(
            ((down_hbm, down), (up_hbm, up), (key_hbm, keys), (value_hbm, values))
        )
    ]
    barrier = pltpu.get_barrier_semaphore()
    for off in range(1, replicas):
        pl.semaphore_signal(
            barrier, inc=1, device_id={"replica": lax.rem(me + off, replicas)},
            device_id_type=pl.DeviceIdType.MESH,
        )
    pl.semaphore_signal(
        barrier, inc=1, device_id={"tensor": 1 - core}, device_id_type=pl.DeviceIdType.MESH
    )
    for load in loads:
        load.start()

    adapter_col = to_column(adapter_ref[...], rows)
    pool_row = pool_ref[...]
    pool_size = pool_row.shape[1]
    hits = adapter_col == iota((rows, pool_size), 1)
    index_col = jnp.sum(jnp.where(hits, pool_row, 0), axis=1, keepdims=True)
    owner_col = index_col // holding
    local_col = index_col - owner_col * holding
    owner_row = to_row(owner_col, rows)
    local_row = to_row(local_col, rows)
    same = owner_col == owner_row
    before_i = iota((rows, rows), 1) < iota((rows, rows), 0)
    before_j = iota((rows, rows), 0) < iota((rows, rows), 1)
    place_col = jnp.sum(jnp.where(same & before_i, 1, 0), axis=1, keepdims=True)
    place_row = jnp.sum(jnp.where(same & before_j, 1, 0), axis=0, keepdims=True)

    at_row = iota((slots, rows), 0)
    piece_of = (iota((slots, 1), 0) % TILE) // cap
    step = min(piece_width, 512)

    def fill(number):
        pick = (owner_row == at_row // TILE) & (place_row == at_row % cap + number * cap)
        pick_pieces = jnp.concatenate(
            [
                jnp.where(pick & ((at_row % TILE) // cap == h), 1.0, 0.0).astype(BF16)
                for h in range(pieces)
            ],
            axis=1,
        )
        local_slot = jnp.sum(jnp.where(pick, local_row + 1, 0), axis=1, keepdims=True) - 1
        for start in range(0, piece_width, step):
            stacked = jnp.concatenate(
                [
                    hidden_ref[:, h * piece_width + start:h * piece_width + start + step]
                    for h in range(pieces)
                ],
                axis=0,
            )
            taken = jnp.dot(pick_pieces, stacked, preferred_element_type=F32)
            send_rows[number, :, :, start:start + step] = taken.astype(BF16).reshape(
                replicas, TILE, step
            )
        send_rows[number, :, :, piece_width:] = jnp.broadcast_to(
            local_slot.astype(F32), (slots, LANES)
        ).astype(BF16).reshape(replicas, TILE, LANES)

    half = piece_width // 2
    spans = ((0, half), (half, piece_width + LANES))

    def exchange(number, source, target, send_sem, recv_sem, span=None, lane=None):
        copies = []
        lane = number if lane is None else lane
        span = (0, source.shape[3]) if span is None else span
        columns = slice(*span)
        order = sorted(range(1, replicas), key=lambda off: -abs(off - replicas // 2))
        for off in order:
            there = lax.rem(me + off, replicas)
            copy = pltpu.make_async_remote_copy(
                src_ref=source.at[number, there, :, columns],
                dst_ref=target.at[number, me, :, columns],
                send_sem=send_sem.at[lane, off], recv_sem=recv_sem.at[lane, off],
                device_id={"replica": there}, device_id_type=pl.DeviceIdType.MESH,
            )
            copy.start()
            copies.append(copy)
        target[number, me, :, columns] = source[number, me, :, columns]
        return copies

    per_tile = LANES // rank_width
    tiles = holding * rank_width // LANES
    lane_adapter = (iota((slots, LANES), 1) // rank_width).astype(F32)
    row_at = iota((slots, 1), 0)

    def shrink_part(number):
        terms = [None] * pieces
        for at, span in enumerate(((0, half), (half, piece_width))):
            for copy in row_copies[2 * number + at]:
                copy.wait_recv()
            for h in range(pieces):
                term = lax.dot_general(
                    got_rows[number, :, :, span[0]:span[1]].reshape(slots, half),
                    down[:, h * piece_width + span[0]:h * piece_width + span[1]],
                    (((1,), (1,)), ((), ())), preferred_element_type=F32,
                )
                terms[h] = term if terms[h] is None else terms[h] + term
        partial_sum = terms[0]
        for h in range(1, pieces):
            partial_sum = jnp.where(piece_of == h, terms[h], partial_sum)
        local = got_rows[number, :, :, piece_width:].reshape(slots, LANES).astype(F32)
        folded = jnp.zeros((slots, LANES), F32)
        for tile in range(tiles):
            keep = local == lane_adapter + tile * per_tile
            folded += jnp.where(keep, partial_sum[:, tile * LANES:(tile + 1) * LANES], 0.0)
        shift = rank_width
        while shift < LANES:
            folded = folded + pltpu.roll(folded, shift, 1)
            shift *= 2
        shift = cap
        while shift < TILE:
            upper = (row_at // shift) % 2 == 1
            folded = folded + jnp.where(
                upper, pltpu.roll(folded, shift, 0), pltpu.roll(folded, slots - shift, 0)
            )
            shift *= 2
        part[number] = folded
        swap = pltpu.make_async_remote_copy(
            src_ref=part.at[number], dst_ref=other_part.at[number],
            send_sem=part_sem.at[number, 0], recv_sem=part_sem.at[number, 1],
            device_id={"tensor": 1 - core}, device_id_type=pl.DeviceIdType.MESH,
        )
        swap.start()
        return swap

    def expand_part(number):
        local = got_rows[number, :, :, piece_width:].reshape(slots, LANES).astype(F32)
        shrink = (part[number] + other_part[number]).astype(BF16).astype(F32)
        wide = jnp.concatenate(
            [
                jnp.where(local == lane_adapter + tile * per_tile, shrink, 0.0).astype(BF16)
                for tile in range(tiles)
            ],
            axis=1,
        )
        wide_step = min(delta_width, 512)
        for start in range(0, delta_width, wide_step):
            taken = None
            for h in range(pieces):
                found = jnp.dot(
                    wide, up[:, h * delta_width + start:h * delta_width + start + wide_step],
                    preferred_element_type=F32,
                )
                taken = found if taken is None else jnp.where(piece_of == h, found, taken)
            send_delta[number, :, :, start:start + wide_step] = taken.astype(BF16).reshape(
                replicas, TILE, wide_step
            )

    fill(0)
    pl.semaphore_wait(barrier, replicas)
    row_copies = []
    for number in range(parts):
        if number:
            fill(number)
        for at, span in enumerate(spans):
            row_copies.append(
                exchange(number, send_rows, got_rows, row_send, row_recv, span, 2 * number + at)
            )
    delta_copies, swaps = [], []
    for number in range(parts):
        if number == 0:
            loads[0].wait()
        swap = shrink_part(number)
        if number == 0:
            loads[1].wait()
        swap.wait_recv()
        swaps.append(swap)
        expand_part(number)
        delta_copies.append(exchange(number, send_delta, got_delta, delta_send, delta_recv))

    at_col = iota((rows, slots), 1)
    loads[2].wait()
    loads[3].wait()
    deltas = [None] * pieces
    for number in range(parts):
        mine = (owner_col == at_col // TILE) & (place_col == at_col % cap + number * cap)
        for copy in delta_copies[number]:
            copy.wait_recv()
        for h in range(pieces):
            back = jnp.where(mine & ((at_col % TILE) // cap == h), 1.0, 0.0).astype(BF16)
            found = jnp.dot(
                back, got_delta[number].reshape(slots, delta_width), preferred_element_type=F32
            )
            deltas[h] = found if deltas[h] is None else deltas[h] + found
    for h in range(pieces):
        columns = slice(h * delta_width, (h + 1) * delta_width)
        query[:, columns] = (base_ref[:, columns].astype(F32) + deltas[h]).astype(BF16).astype(F32)
    for copy in sum(row_copies, []) + sum(delta_copies, []) + swaps:
        copy.wait_send()

    cache_len, kv_width = keys.shape[1:]
    kv_heads = kv_width // HEAD_WIDTH
    heads = out_width // HEAD_WIDTH
    group = heads // kv_heads
    block = 8
    tall = heads * block
    request_of = iota((tall, 1), 0) % block
    kv_of_row = iota((tall, 1), 0) // (group * block)
    length_col = to_column(length_ref[...], rows)
    position = iota((block, cache_len), 1)

    def attend(first):
        loaded = query[first:first + block, :]
        stacked = jnp.concatenate(
            [loaded[:, at * HEAD_WIDTH:(at + 1) * HEAD_WIDTH] for at in range(heads)], axis=0
        )
        spread = jnp.concatenate(
            [jnp.where(kv_of_row == kv, stacked, 0.0).astype(BF16) for kv in range(kv_heads)],
            axis=1,
        )
        scores = None
        for at in range(block):
            found = lax.dot_general(
                spread, keys[first + at], (((1,), (1,)), ((), ())), preferred_element_type=F32
            )
            scores = found if scores is None else jnp.where(request_of == at, found, scores)
        valid = position < length_col[first:first + block, :]
        bias = jnp.where(valid, 0.0, -1e30).astype(F32)
        valid_all = jnp.concatenate([bias] * heads, axis=0)
        scores = jnp.where(valid_all < 0.0, -1e30, scores * (HEAD_WIDTH ** -0.5))
        expo = jnp.exp(scores - jnp.max(scores, axis=1, keepdims=True))
        weights = expo / jnp.sum(expo, axis=1, keepdims=True)
        total = jnp.zeros((tall, kv_width), F32)
        for at in range(block):
            chosen = jnp.where(request_of == at, weights, 0.0).astype(BF16)
            total += jnp.dot(chosen, values[first + at], preferred_element_type=F32)
        return [
            total[at * block:(at + 1) * block,
                  (at // group) * HEAD_WIDTH:(at // group + 1) * HEAD_WIDTH]
            for at in range(heads)
        ]

    for first in range(0, rows, 2 * block):
        low, high = attend(first), attend(first + block)
        for at in range(heads):
            out_ref[first:first + 2 * block, at * HEAD_WIDTH:(at + 1) * HEAD_WIDTH] = (
                jnp.concatenate([low[at], high[at]], axis=0).astype(BF16)
            )


def local_step(
    replicas, hidden, base, down, up, request_adapter, adapter_pool_row, keys, values, lengths
):
    holding, rank_width, out_width = up.shape
    rows, width = hidden.shape
    parts = min(PARTS, 2 * rows // replicas)
    cap = 2 * rows // replicas // parts
    pieces = TILE // cap
    slots = replicas * TILE
    down_rows = jnp.swapaxes(down, 1, 2).reshape(holding * rank_width, width)
    up_rows = up.reshape(holding * rank_width, out_width)
    vmem = pl.BlockSpec(memory_space=pltpu.VMEM)
    hbm = pl.BlockSpec(memory_space=pl.ANY)
    return pl.pallas_call(
        functools.partial(kernel, replicas, holding, rank_width),
        out_shape=jax.ShapeDtypeStruct((rows, out_width), BF16),
        in_specs=[vmem] * 5 + [hbm] * 4,
        out_specs=vmem,
        scratch_shapes=[
            pltpu.VMEM(down_rows.shape, BF16),
            pltpu.VMEM(up_rows.shape, BF16),
            pltpu.VMEM(keys.shape, BF16),
            pltpu.VMEM(values.shape, BF16),
            pltpu.VMEM((parts, replicas, TILE, width // pieces + LANES), BF16),
            pltpu.VMEM((parts, replicas, TILE, width // pieces + LANES), BF16),
            pltpu.VMEM((parts, slots, LANES), F32),
            pltpu.VMEM((parts, slots, LANES), F32),
            pltpu.VMEM((parts, replicas, TILE, out_width // pieces), BF16),
            pltpu.VMEM((parts, replicas, TILE, out_width // pieces), BF16),
            pltpu.VMEM((rows, out_width), F32),
            pltpu.SemaphoreType.DMA((4,)),
            pltpu.SemaphoreType.DMA((2 * parts, replicas)),
            pltpu.SemaphoreType.DMA((2 * parts, replicas)),
            pltpu.SemaphoreType.DMA((parts, 2)),
            pltpu.SemaphoreType.DMA((parts, replicas)),
            pltpu.SemaphoreType.DMA((parts, replicas)),
        ],
        compiler_params=pltpu.CompilerParams(
            collective_id=0, has_side_effects=True, vmem_limit_bytes=63 * 1024 * 1024
        ),
        name="adapter_attention",
    )(
        hidden, base, request_adapter.reshape(1, rows),
        adapter_pool_row.reshape(1, adapter_pool_row.shape[0]), lengths.reshape(1, rows),
        down_rows, up_rows, keys, values,
    )


def solution(mesh):
    return jax.shard_map(
        functools.partial(local_step, mesh.shape["replica"]),
        mesh=mesh,
        in_specs=(
            P(("groups", "replica"), "tensor"),
            P(("groups", "replica"), "tensor"),
            P(("groups", "replica"), "tensor", None),
            P(("groups", "replica"), None, "tensor"),
            P(("groups", "replica")),
            P("groups"),
            P(("groups", "replica"), None, "tensor"),
            P(("groups", "replica"), None, "tensor"),
            P(("groups", "replica")),
        ),
        out_specs=P(("groups", "replica"), "tensor"),
        check_vma=False,
    )
```
